512 devices in a mesh: src: 16 (over x, z_hi, core), rcv: 32 (over z_lo, y).
Axes of the slice: x: 4, y: 4, z: 16 (z_hi: 2, z_lo: 8; z = z_hi * 8 + z_lo), core: 2. Of those that a mesh axis runs over, the one named last changes fastest.
Arguments:
- source_spectra: bfloat16 [32, 8, 23, 2, 8, 4096], P('rcv', None, None, None, None, 'src'), may hold values from -6 to 6
- receiver_spectra: bfloat16 [16, 8, 23, 2, 8, 8192], P('src', None, None, None, None, 'rcv'), may hold values from -6 to 6
Outputs:
- cross_stack: bfloat16 [2, 8, 4096, 8192], P(None, None, 'src', 'rcv')
The draws below stay inside these ranges and needn't reach their ends.
All inputs are finite; a program needn't handle non-finite values.
Results may differ from the reference program's by a relative error of at most 0.0058.
Values may be sent and summed in bfloat16 or wider, within the bound.
No kernel may reach another device: no remote copies, remote signals or barrier semaphores. Data moves between devices by JAX's collectives and lax.ppermute only.
A program may use at most 64 MiB of HBM per device.

```python
import jax
import jax.numpy as jnp
from jax import lax

CB = 256
WB = 23
NB = 8
STEPS = 8
NS_CH = 4096
NR_CH = 8192
N_SRC = 16
N_RCV = 32


def level_of(rng, dims, pieces, low, high):
    level = 1.0
    for position, blocks in pieces:
        steps = jax.random.uniform(jax.random.fold_in(jax.random.fold_in(rng, 6), position), (blocks,), jnp.float32, low / len(pieces), high / len(pieces))
        level = level * jnp.repeat(jnp.exp(steps), dims[position] // blocks).reshape((-1,) + (1,) * (len(dims) - 1 - position))
    return level


def normal_values(own_key, extent, width, bound, split=(), held_as=jnp.bfloat16):
    values = jax.random.normal(own_key, extent, jnp.float32) * width
    if len(split) > 0:
        values = level_of(own_key, extent, split, -0.22, 0.18) * values
    return jnp.clip(values, min=-bound, max=bound).astype(held_as)


def setup_inputs(seed: int = 0) -> dict:
    key_list = jax.random.split(jax.random.key(seed), 3)
    return {
        "source_spectra": normal_values(key_list[0], (N_RCV, STEPS, WB, 2, NB, NS_CH), 1.0, 6.0, ((0, 32), (5, 16))),
        "receiver_spectra": normal_values(key_list[1], (N_SRC, STEPS, WB, 2, NB, NR_CH), 1.0, 6.0, ((0, 16), (5, 32))),
    }


def whiten(spectra):
    values = spectra.astype(jnp.float32)
    power_sum = lax.optimization_barrier(jnp.sum(values * values, axis=3, keepdims=True))
    mean_level = lax.optimization_barrier(jnp.mean(power_sum, axis=4, keepdims=True))
    return (values / jnp.sqrt(0.5 * power_sum + 0.5 * mean_level + 0.25)).astype(jnp.bfloat16)

def reference(source_spectra, receiver_spectra):
    source_white = whiten(source_spectra)
    receiver_white = whiten(receiver_spectra)
    step_ids = jnp.arange(STEPS, dtype=jnp.int32)
    block_ids = jnp.arange(N_SRC, dtype=jnp.int32)

    def one_column(column):
        source_rows = source_white[(column + step_ids) % N_RCV, step_ids]
        source_rows = source_rows.astype(jnp.float32).reshape(STEPS, WB, 2, NB, N_SRC, CB)
        receiver_cols = lax.dynamic_slice_in_dim(receiver_white, column * CB, CB, axis=5)
        receiver_cols = receiver_cols[(block_ids[:, None] + step_ids[None, :]) % N_SRC, step_ids[None, :]]
        receiver_cols = receiver_cols.astype(jnp.float32)
        src_real = source_rows[:, :, 0]
        src_imag = source_rows[:, :, 1]
        rcv_real = receiver_cols[:, :, :, 0]
        rcv_imag = receiver_cols[:, :, :, 1]
        real_part = jnp.einsum('twbip,itwbq->bipq', src_real, rcv_real) + jnp.einsum('twbip,itwbq->bipq', src_imag, rcv_imag)
        imag_part = jnp.einsum('twbip,itwbq->bipq', src_imag, rcv_real) - jnp.einsum('twbip,itwbq->bipq', src_real, rcv_imag)
        return jnp.stack([real_part, imag_part])
    columns = lax.map(one_column, jnp.arange(N_RCV, dtype=jnp.int32))
    stacked = columns.transpose(1, 2, 3, 4, 0, 5).reshape(2, NB, N_SRC * CB, N_RCV * CB)
    return (stacked * (STEPS * WB) ** (-0.5)).astype(jnp.bfloat16)
```

```python
import jax
import jax.numpy as jnp
from jax import lax
from jax.sharding import PartitionSpec as P


def from_ahead(block, axis, distance):
    size = lax.axis_size(axis)
    return lax.ppermute(block, axis, [((i + distance) % size, i) for i in range(size)])


def whiten(spectra):
    values = spectra.astype(jnp.float32)
    power = jnp.sum(values * values, axis=-3, keepdims=True)
    level = jnp.mean(power, axis=-2, keepdims=True)
    return (values / jnp.sqrt(0.5 * power + 0.5 * level + 0.25)).astype(jnp.bfloat16)


def cross_terms(source_slots, receiver_slots):
    left = jnp.stack([whiten(s) for s in source_slots])
    right = jnp.stack([whiten(r) for r in receiver_slots])
    bins, width = left.shape[-2:]
    turned = jnp.concatenate([left[:, :, 1:2], -left[:, :, 0:1]], axis=2)
    both = jnp.concatenate([left, turned], axis=-1).reshape(-1, bins, 2 * width)
    right = right.reshape(-1, bins, width)
    return jnp.einsum("kbp,kbq->bpq", both, right, preferred_element_type=jnp.float32)


def body(source_spectra, receiver_spectra):
    source, receiver = source_spectra[0], receiver_spectra[0]
    groups, windows = source.shape[:2]
    width = source.shape[-1]
    source_slots = [source[0]]
    receiver_slots = [receiver[0]]
    source_slots += [from_ahead(source[t], "rcv", t) for t in range(1, groups)]
    receiver_slots += [from_ahead(receiver[t], "src", t) for t in range(1, groups)]
    total = cross_terms(source_slots, receiver_slots)
    stacked = jnp.stack([total[:, :width], total[:, width:]])
    return (stacked * (groups * windows) ** (-0.5)).astype(jnp.bfloat16)


def solution(mesh):
    return jax.shard_map(
        body,
        mesh=mesh,
        in_specs=(P("rcv", None, None, None, None, "src"), P("src", None, None, None, None, "rcv")),
        out_specs=P(None, None, "src", "rcv"),
        check_vma=False,
    )
```

```python
import functools

import jax
import jax.numpy as jnp
from jax import lax
from jax.experimental import pallas as pl
from jax.experimental.pallas import tpu as pltpu
from jax.sharding import PartitionSpec as P


LANES = 128


def whiten_slot(slot_ref, first, out_ref, turned_ref=None):
    windows, parts, bins, width = slot_ref.shape

    def put(ref, row, values):
        for h in range(width // LANES):
            ref[h, pl.ds(row, bins), :] = values[:, h * LANES:(h + 1) * LANES]

    def one_window(w, carry):
        values = slot_ref[w].astype(jnp.float32)
        re, im = values[0], values[1]
        power = re * re + im * im
        level = jnp.mean(power, axis=0, keepdims=True)
        gain = lax.rsqrt(0.5 * power + 0.5 * level + 0.25)
        re, im = re * gain, im * gain
        row = pl.multiple_of(first + w * parts * bins, bins)
        put(out_ref, row, re)
        put(out_ref, row + bins, im)
        if turned_ref is not None:
            put(turned_ref, row, im)
            put(turned_ref, row + bins, -re)
        return carry

    lax.fori_loop(0, windows, one_window, 0, unroll=True)


def of_bin(ref, b, first, rows, bins):
    halves = [ref[h, pl.ds(first * bins + b, rows, stride=bins), :] for h in range(ref.shape[0])]
    return jnp.concatenate(halves, axis=-1)


def early_kernel(count, *refs):
    slots, (acc, left, u, t, v) = refs[:-5], refs[-5:]
    sources, receivers = slots[:count], slots[count:]
    windows, parts, bins, width = slots[0].shape
    slot_rows = windows * parts
    for k, ref in enumerate(sources):
        whiten_slot(ref, k * slot_rows * bins, u, t)
    for k, ref in enumerate(receivers):
        whiten_slot(ref, k * slot_rows * bins, v)
    met = len(receivers) * slot_rows
    rest = (len(sources) - len(receivers)) * slot_rows
    for b in range(bins):
        right = of_bin(v, b, 0, met, bins).astype(jnp.bfloat16)
        for part, ref in enumerate((u, t)):
            now = of_bin(ref, b, 0, met, bins).astype(jnp.bfloat16)
            acc[b, part * width:(part + 1) * width, :] = lax.dot_general(
                now, right, (((0,), (0,)), ((), ())), preferred_element_type=jnp.float32
            )
            later = of_bin(ref, b, met, rest, bins)
            left[b, part * width:(part + 1) * width, :] = later.T.astype(jnp.bfloat16)


def late_kernel(scale, count, *refs):
    slots = [ref.at[k] for ref in refs[:count] for k in range(ref.shape[0])]
    acc, left, out_hbm, v, block, out_sem = refs[count:]
    windows, parts, bins, width = slots[0].shape
    slot_rows = windows * parts
    for k, ref in enumerate(slots):
        whiten_slot(ref, k * slot_rows * bins, v)
    stores = []
    for b in range(bins):
        right = of_bin(v, b, 0, len(slots) * slot_rows, bins).astype(jnp.bfloat16)
        total = acc[b] + jnp.dot(left[b], right, preferred_element_type=jnp.float32)
        total = (total * scale).astype(jnp.bfloat16)
        block[0, b] = total[:width]
        block[1, b] = total[width:]
        for part in range(2):
            copy = pltpu.make_async_copy(block.at[part, b], out_hbm.at[part, b], out_sem.at[part, b])
            copy.start()
            stores.append(copy)
    for copy in stores:
        copy.wait()


def early(sources, receivers):
    windows, parts, bins, width = sources[0].shape
    slot_rows = windows * parts
    met = len(receivers) * slot_rows
    rest = (len(sources) - len(receivers)) * slot_rows
    vmem = pl.BlockSpec(memory_space=pltpu.VMEM)
    lanes = width // LANES
    return pl.pallas_call(
        functools.partial(early_kernel, len(sources)),
        out_shape=(
            jax.ShapeDtypeStruct((bins, 2 * width, width), jnp.float32),
            jax.ShapeDtypeStruct((bins, 2 * width, rest), jnp.bfloat16),
        ),
        in_specs=[vmem] * (len(sources) + len(receivers)),
        out_specs=(vmem, vmem),
        scratch_shapes=[
            pltpu.VMEM((lanes, (met + rest) * bins, LANES), jnp.float32),
            pltpu.VMEM((lanes, (met + rest) * bins, LANES), jnp.float32),
            pltpu.VMEM((lanes, met * bins, LANES), jnp.float32),
        ],
        compiler_params=pltpu.CompilerParams(vmem_limit_bytes=40 * 2**20),
        cost_estimate=pl.CostEstimate(flops=1_000_000, bytes_accessed=1_000_000, transcendentals=0),
    )(*sources, *receivers)


def late(receivers, acc, left, scale):
    windows, parts, bins, width = receivers[0].shape[1:]
    vmem = pl.BlockSpec(memory_space=pltpu.VMEM)
    hbm = pl.BlockSpec(memory_space=pl.ANY)
    return pl.pallas_call(
        functools.partial(late_kernel, scale, len(receivers)),
        out_shape=jax.ShapeDtypeStruct((2, bins, width, width), jnp.bfloat16),
        in_specs=[vmem] * (len(receivers) + 2),
        out_specs=hbm,
        scratch_shapes=[
            pltpu.VMEM((width // LANES, left.shape[-1] * bins, LANES), jnp.float32),
            pltpu.VMEM((2, bins, width, width), jnp.bfloat16),
            pltpu.SemaphoreType.DMA((2, bins)),
        ],
        compiler_params=pltpu.CompilerParams(vmem_limit_bytes=40 * 2**20),
        cost_estimate=pl.CostEstimate(flops=200_000_000, bytes_accessed=9_000_000, transcendentals=200_000),
    )(*receivers, acc, left)


def pack_kernel(place_ref, source, z, p, q, y1, y2, y3, y4):
    place = place_ref[0, 0]
    pairs = (None, y1, y2, y3)
    for t in range(1, 8):
        out = y4 if t == 4 else pairs[t % 4].at[t // 4]

        def put(cond, ref, index, out=out):
            @pl.when(cond)
            def _():
                out[...] = ref[index]

        if t <= 3:
            put(place >= t, source, t)
        put((place < t) & (place >= t - 4), z, jnp.clip(t - 1 - place, 0, 3))
        if t in (5, 6):
            put(place == 0, p, t - 5)
        if t in (6, 7):
            put(place == 1, p, t - 6)
        if t == 7:
            put((place == 0) | (place == 2), q, 0)


def pack(place, source, z, p, q):
    slot = jax.ShapeDtypeStruct(source.shape[1:], source.dtype)
    two = jax.ShapeDtypeStruct((2,) + source.shape[1:], source.dtype)
    vmem = pl.BlockSpec(memory_space=pltpu.VMEM)
    return pl.pallas_call(
        pack_kernel,
        out_shape=(two, two, two, slot),
        in_specs=[pl.BlockSpec(memory_space=pltpu.SMEM)] + [vmem] * 4,
        out_specs=(vmem,) * 4,
        compiler_params=pltpu.CompilerParams(vmem_limit_bytes=24 * 2**20),
        cost_estimate=pl.CostEstimate(flops=60_000_000_000, bytes_accessed=6_000_000, transcendentals=0),
    )(place.astype(jnp.int32).reshape(1, 1), source, z, p, q)


PLAN = (
    ("send", "Cl"),
    ("send", "D"),
    ("send", "X6"),
    ("send", "X2"),
    ("send", "Q"),
    ("send", "P"),
    ("send", "Z"),
    ("after", "X2"),
    ("send", "O"),
    ("after", "P"),
    ("after", "Q"),
    ("after", "Z"),
    ("send", "F"),
    ("send", "Y1"),
    ("send", "Y2"),
    ("send", "Y3"),
)


def body(source_spectra, receiver_spectra):
    source, receiver = source_spectra[0], receiver_spectra[0]
    groups, windows = source.shape[:2]
    core = lax.axis_index("src") % 2
    place = lax.axis_index("rcv") % 4
    got, held = {}, {}

    def of_core(zero, one):
        return jnp.where(core == 0, zero, one)

    def pair(b):
        if not held:
            held["y"] = pack(place, source, got["Z"], got["P"], got["Q"][None])
        return held["y"][b - 1]

    def low(far):
        return of_core(receiver[1], receiver[3]) if far else of_core(receiver[3], receiver[1])

    def high(far):
        return of_core(receiver[5], receiver[7]) if far else of_core(receiver[7], receiver[5])

    def back(steps):
        return [(i, (i - steps(i)) % 16) for i in range(16)]

    def back_z(steps, places=range(4)):
        return [(i, (i - 4 * steps) % 32) for i in range(32) if i % 4 in places]

    def back_y(steps):
        return [(i, i // 4 * 4 + (i % 4 - steps) % 4) for i in range(32)]

    moves = {
        "Cl": ("src", [(i, i ^ 1) for i in range(16)], lambda: low(True)),
        "D": ("src", [(i, (i - 4) % 16 ^ 1) for i in range(16)], lambda: high(True)),
        "X6": ("src", back(lambda i: 4), lambda: receiver[6]),
        "X2": ("src", back(lambda i: 4), lambda: jnp.stack([receiver[4], high(False)])),
        "O": ("src", back(lambda i: 3 - 2 * (i % 2)), lambda: jnp.stack([low(False), got["X2"][1]])),
        "F": ("src", back(lambda i: 2), lambda: jnp.stack([receiver[2], got["X6"], got["Cl"], got["D"]])),
        "Z": ("rcv", back_z(1), lambda: lax.dynamic_slice_in_dim(source, 1 + place, 4, 0)),
        "P": ("rcv", back_z(2, (0, 1)), lambda: lax.dynamic_slice_in_dim(source, jnp.minimum(5 + place, 6), 2, 0)),
        "Q": ("rcv", back_z(2, (0, 2)), lambda: source[7]),
        "Y1": ("rcv", back_y(1), lambda: pair(1)),
        "Y2": ("rcv", back_y(2), lambda: pair(2)),
        "Y3": ("rcv", back_y(3), lambda: pair(3)),
    }
    tied = []
    for act, name in PLAN:
        if act == "after":
            tied.append(name)
            continue
        axis, route, make = moves[name]
        block = make()
        if tied:
            block, *arrived = lax.optimization_barrier((block, *[got[n] for n in tied]))
            got.update(zip(tied, arrived))
        got[name] = lax.ppermute(block, axis, route)
    y1, y2, y3 = got["Y1"], got["Y2"], got["Y3"]
    sources = [source[0], held["y"][3], of_core(y1[0], y3[0]), of_core(y1[1], y3[1])]
    sources += [y2[0], y2[1], of_core(y3[0], y1[0]), of_core(y3[1], y1[1])]
    acc, left = early(sources, [receiver[0], got["X2"][0], got["O"][0], got["O"][1]])
    return late([got["F"]], acc, left, (groups * windows) ** (-0.5))


def solution(mesh):
    return jax.shard_map(
        body,
        mesh=mesh,
        in_specs=(P("rcv", None, None, None, None, "src"), P("src", None, None, None, None, "rcv")),
        out_specs=P(None, None, "src", "rcv"),
        check_vma=False,
    )
```

```python
import functools

import jax
import jax.numpy as jnp
from jax import lax
from jax.experimental import pallas as pl
from jax.experimental.pallas import tpu as pltpu
from jax.sharding import PartitionSpec as P


LANES = 128


def whiten_slot(slot_ref, first, out_ref, turned_ref=None):
    windows, parts, bins, width = slot_ref.shape

    def put(ref, row, values):
        for h in range(width // LANES):
            ref[h, pl.ds(row, bins), :] = values[:, h * LANES:(h + 1) * LANES]

    def one_window(w, carry):
        values = slot_ref[w].astype(jnp.float32)
        re, im = values[0], values[1]
        power = re * re + im * im
        level = jnp.mean(power, axis=0, keepdims=True)
        gain = lax.rsqrt(0.5 * power + 0.5 * level + 0.25)
        re, im = re * gain, im * gain
        row = pl.multiple_of(first + w * parts * bins, bins)
        put(out_ref, row, re)
        put(out_ref, row + bins, im)
        if turned_ref is not None:
            put(turned_ref, row, im)
            put(turned_ref, row + bins, -re)
        return carry

    lax.fori_loop(0, windows, one_window, 0, unroll=True)


def of_bin(ref, b, first, rows, bins):
    halves = [ref[h, pl.ds(first * bins + b, rows, stride=bins), :] for h in range(ref.shape[0])]
    return jnp.concatenate(halves, axis=-1)


def early_kernel(count, *refs):
    slots, (acc, left, u, t, v) = refs[:-5], refs[-5:]
    sources, receivers = slots[:count], slots[count:]
    windows, parts, bins, width = slots[0].shape
    slot_rows = windows * parts
    for k, ref in enumerate(sources):
        whiten_slot(ref, k * slot_rows * bins, u, t)
    for k, ref in enumerate(receivers):
        whiten_slot(ref, k * slot_rows * bins, v)
    met = len(receivers) * slot_rows
    rest = (len(sources) - len(receivers)) * slot_rows
    for b in range(bins):
        right = of_bin(v, b, 0, met, bins).astype(jnp.bfloat16)
        for part, ref in enumerate((u, t)):
            now = of_bin(ref, b, 0, met, bins).astype(jnp.bfloat16)
            acc[b, part * width:(part + 1) * width, :] = lax.dot_general(
                now, right, (((0,), (0,)), ((), ())), preferred_element_type=jnp.float32
            )
            later = of_bin(ref, b, met, rest, bins)
            left[b, part * width:(part + 1) * width, :] = later.T.astype(jnp.bfloat16)


def late_kernel(scale, count, *refs):
    slots = [ref.at[k] for ref in refs[:count] for k in range(ref.shape[0])]
    acc, left, out_hbm, v, block, out_sem = refs[count:]
    windows, parts, bins, width = slots[0].shape
    slot_rows = windows * parts
    for k, ref in enumerate(slots):
        whiten_slot(ref, k * slot_rows * bins, v)
    stores = []
    for b in range(bins):
        right = of_bin(v, b, 0, len(slots) * slot_rows, bins).astype(jnp.bfloat16)
        total = acc[b] + jnp.dot(left[b], right, preferred_element_type=jnp.float32)
        total = (total * scale).astype(jnp.bfloat16)
        block[0, b] = total[:width]
        block[1, b] = total[width:]
        for part in range(2):
            copy = pltpu.make_async_copy(block.at[part, b], out_hbm.at[part, b], out_sem.at[part, b])
            copy.start()
            stores.append(copy)
    for copy in stores:
        copy.wait()


def early(sources, receivers):
    windows, parts, bins, width = sources[0].shape
    slot_rows = windows * parts
    met = len(receivers) * slot_rows
    rest = (len(sources) - len(receivers)) * slot_rows
    vmem = pl.BlockSpec(memory_space=pltpu.VMEM)
    lanes = width // LANES
    return pl.pallas_call(
        functools.partial(early_kernel, len(sources)),
        out_shape=(
            jax.ShapeDtypeStruct((bins, 2 * width, width), jnp.float32),
            jax.ShapeDtypeStruct((bins, 2 * width, rest), jnp.bfloat16),
        ),
        in_specs=[vmem] * (len(sources) + len(receivers)),
        out_specs=(vmem, vmem),
        scratch_shapes=[
            pltpu.VMEM((lanes, (met + rest) * bins, LANES), jnp.float32),
            pltpu.VMEM((lanes, (met + rest) * bins, LANES), jnp.float32),
            pltpu.VMEM((lanes, met * bins, LANES), jnp.float32),
        ],
        compiler_params=pltpu.CompilerParams(vmem_limit_bytes=40 * 2**20),
        cost_estimate=pl.CostEstimate(flops=1_000_000, bytes_accessed=1_000_000, transcendentals=0),
    )(*sources, *receivers)


def late(receivers, acc, left, scale):
    windows, parts, bins, width = receivers[0].shape[1:]
    vmem = pl.BlockSpec(memory_space=pltpu.VMEM)
    hbm = pl.BlockSpec(memory_space=pl.ANY)
    return pl.pallas_call(
        functools.partial(late_kernel, scale, len(receivers)),
        out_shape=jax.ShapeDtypeStruct((2, bins, width, width), jnp.bfloat16),
        in_specs=[vmem] * (len(receivers) + 2),
        out_specs=hbm,
        scratch_shapes=[
            pltpu.VMEM((width // LANES, left.shape[-1] * bins, LANES), jnp.float32),
            pltpu.VMEM((2, bins, width, width), jnp.bfloat16),
            pltpu.SemaphoreType.DMA((2, bins)),
        ],
        compiler_params=pltpu.CompilerParams(vmem_limit_bytes=40 * 2**20),
        cost_estimate=pl.CostEstimate(flops=200_000_000, bytes_accessed=9_000_000, transcendentals=200_000),
    )(*receivers, acc, left)


def pack_kernel(place_ref, source, z, p, y1, y2, y3, y4):
    place = place_ref[0, 0]
    pairs = (None, y1, y2, y3)
    for t in range(1, 8):
        out = y4 if t == 4 else pairs[t % 4].at[t // 4]

        def put(cond, ref, index, out=out):
            @pl.when(cond)
            def _():
                out[...] = ref[index]

        aside = {6: place == 0, 7: place == 2}.get(t, False)
        if t <= 3:
            put(place >= t, source, t)
        put((place < t) & (place >= t - 4), z, jnp.clip(t - 1 - place, 0, 3))
        if t in (6, 7):
            put(aside, source, t)
        if t in (5, 7):
            put(place == 0, p, t // 7)
        if t in (6, 7):
            put(place == 1, p, t - 6)


def pack(place, source, z, p):
    slot = jax.ShapeDtypeStruct(source.shape[1:], source.dtype)
    two = jax.ShapeDtypeStruct((2,) + source.shape[1:], source.dtype)
    vmem = pl.BlockSpec(memory_space=pltpu.VMEM)
    return pl.pallas_call(
        pack_kernel,
        out_shape=(two, two, two, slot),
        in_specs=[pl.BlockSpec(memory_space=pltpu.SMEM)] + [vmem] * 3,
        out_specs=(vmem,) * 4,
        compiler_params=pltpu.CompilerParams(vmem_limit_bytes=24 * 2**20),
        cost_estimate=pl.CostEstimate(flops=1_000, bytes_accessed=1_000, transcendentals=0),
    )(place.astype(jnp.int32).reshape(1, 1), source, z, p)


PLAN = (
    ("send", "W"),
    ("send", "Q"),
    ("send", "P"),
    ("send", "Z"),
    ("after", "Z"),
    ("after", "P"),
    ("after", "Q"),
    ("send", "F"),
)


def body(source_spectra, receiver_spectra):
    source, receiver = source_spectra[0], receiver_spectra[0]
    groups, windows = source.shape[:2]
    core = lax.axis_index("src") % 2
    place = lax.axis_index("rcv") % 4
    got = {}

    def of_core(zero, one):
        return jnp.where(core == 0, zero, one)

    def low(far):
        return of_core(receiver[1], receiver[3]) if far else of_core(receiver[3], receiver[1])

    def high(far):
        return of_core(receiver[5], receiver[7]) if far else of_core(receiver[7], receiver[5])

    def back(steps):
        return [(i, (i - steps(i)) % 16) for i in range(16)]

    def back_z(steps, places=range(4)):
        return [(i, (i - 4 * steps) % 32) for i in range(32) if i % 4 in places]

    def back_y(steps):
        return [(i, i // 4 * 4 + (i % 4 - steps) % 4) for i in range(32)]

    def nothing_like(*shapes):
        return lambda *_: tuple(jnp.zeros(s + receiver.shape[1:], receiver.dtype) for s in shapes)

    def one_x_step(receiver):
        x6 = lax.ppermute(receiver[6], "src", back(lambda i: 4))
        d = lax.ppermute(high(True), "src", [(i, (i - 4) % 16 ^ 1) for i in range(16)])
        return x6, d

    def core_step(receiver):
        return (lax.ppermute(low(True), "src", [(i, i ^ 1) for i in range(16)]),)

    x6, d = lax.cond(core < 2, one_x_step, nothing_like((), ()), receiver)
    (cl,) = lax.cond(core < 2, core_step, nothing_like(()), receiver)
    across_y = [(i, i // 4 * 4 + {0: 2, 2: 3}[i % 4]) for i in range(32) if i % 2 == 0]

    moves = {
        "F": ("src", back(lambda i: 2), lambda: jnp.stack([receiver[2], x6, cl, d])),
        "Z": ("rcv", back_z(1), lambda: lax.dynamic_slice_in_dim(source, 1 + place, 4, 0)),
        "P": ("rcv", back_z(2, (0, 1)), lambda: jnp.stack([jnp.where(place == 0, source[5], source[6]), source[7]])),
        "W": ("rcv", across_y, lambda: jnp.where(place == 0, source[6], source[7])),
        "Q": ("rcv", back_z(2, (2, 3)), lambda: got["W"]),
    }
    tied = []
    for act, name in PLAN:
        if act == "after":
            tied.append(name)
            continue
        axis, route, make = moves[name]
        block = make()
        if tied:
            block, *arrived = lax.optimization_barrier((block, *[got[n] for n in tied]))
            got.update(zip(tied, arrived))
        got[name] = lax.ppermute(block, axis, route)

    def along_y(place, source, receiver, z, p):
        x2 = lax.ppermute(jnp.stack([receiver[4], high(False)]), "src", back(lambda i: 4))
        one, two, three, four = pack(place, source, z, p)
        pairs = [lax.ppermute(x, "rcv", back_y(b)) for b, x in ((1, one), (2, two), (3, three))]
        near = jnp.stack([low(False), x2[1]])
        near = lax.ppermute(near, "src", back(lambda i: 3 - 2 * (i % 2)))
        return (*pairs, four, x2[0], near)

    y1, y2, y3, four, x4, near = lax.cond(
        core < 2, along_y, nothing_like((2,), (2,), (2,), (), (), (2,)), place, source, receiver, got["Z"], got["P"]
    )
    two, three = jnp.where(place == 2, got["Q"], y2[1]), jnp.where(place == 3, got["Q"], y3[1])
    sources = [source[0], four, of_core(y1[0], y3[0]), of_core(y1[1], three)]
    sources += [y2[0], two, of_core(y3[0], y1[0]), of_core(three, y1[1])]
    acc, left = early(sources, [receiver[0], x4, near[0], near[1]])
    return late([got["F"]], acc, left, (groups * windows) ** (-0.5))


def solution(mesh):
    return jax.shard_map(
        body,
        mesh=mesh,
        in_specs=(P("rcv", None, None, None, None, "src"), P("src", None, None, None, None, "rcv")),
        out_specs=P(None, None, "src", "rcv"),
        check_vma=False,
    )
```

```python
import functools

import jax
import jax.numpy as jnp
from jax import lax
from jax.experimental import pallas as pl
from jax.experimental.pallas import tpu as pltpu
from jax.sharding import PartitionSpec as P


LANES = 128


def whiten_slot(slot_ref, first, out_ref, turned_ref=None):
    windows, parts, bins, width = slot_ref.shape

    def put(ref, row, values):
        for h in range(width // LANES):
            ref[h, pl.ds(row, bins), :] = values[:, h * LANES:(h + 1) * LANES]

    def one_window(w, carry):
        values = slot_ref[w].astype(jnp.float32)
        re, im = values[0], values[1]
        power = re * re + im * im
        level = jnp.mean(power, axis=0, keepdims=True)
        gain = lax.rsqrt(0.5 * power + 0.5 * level + 0.25)
        re, im = re * gain, im * gain
        row = pl.multiple_of(first + w * parts * bins, bins)
        put(out_ref, row, re)
        put(out_ref, row + bins, im)
        if turned_ref is not None:
            put(turned_ref, row, im)
            put(turned_ref, row + bins, -re)
        return carry

    lax.fori_loop(0, windows, one_window, 0, unroll=True)


def of_bin(ref, b, first, rows, bins):
    halves = [ref[h, pl.ds(first * bins + b, rows, stride=bins), :] for h in range(ref.shape[0])]
    return jnp.concatenate(halves, axis=-1)


def early_kernel(count, *refs):
    slots, (acc, left, u, t, v) = refs[:-5], refs[-5:]
    sources, receivers = slots[:count], slots[count:]
    windows, parts, bins, width = slots[0].shape
    slot_rows = windows * parts
    for k, ref in enumerate(sources):
        whiten_slot(ref, k * slot_rows * bins, u, t)
    for k, ref in enumerate(receivers):
        whiten_slot(ref, k * slot_rows * bins, v)
    met = len(receivers) * slot_rows
    rest = (len(sources) - len(receivers)) * slot_rows
    for b in range(bins):
        right = of_bin(v, b, 0, met, bins).astype(jnp.bfloat16)
        for part, ref in enumerate((u, t)):
            now = of_bin(ref, b, 0, met, bins).astype(jnp.bfloat16)
            acc[b, part * width:(part + 1) * width, :] = lax.dot_general(
                now, right, (((0,), (0,)), ((), ())), preferred_element_type=jnp.float32
            )
            later = of_bin(ref, b, met, rest, bins)
            left[b, part * width:(part + 1) * width, :] = later.T.astype(jnp.bfloat16)


def late_kernel(scale, count, *refs):
    slots = [ref.at[k] for ref in refs[:count] for k in range(ref.shape[0])]
    acc, left, out_hbm, v, block, out_sem = refs[count:]
    windows, parts, bins, width = slots[0].shape
    slot_rows = windows * parts
    for k, ref in enumerate(slots):
        whiten_slot(ref, k * slot_rows * bins, v)
    stores = []
    for b in range(bins):
        right = of_bin(v, b, 0, len(slots) * slot_rows, bins).astype(jnp.bfloat16)
        total = acc[b] + jnp.dot(left[b], right, preferred_element_type=jnp.float32)
        total = (total * scale).astype(jnp.bfloat16)
        block[0, b] = total[:width]
        block[1, b] = total[width:]
        for part in range(2):
            copy = pltpu.make_async_copy(block.at[part, b], out_hbm.at[part, b], out_sem.at[part, b])
            copy.start()
            stores.append(copy)
    for copy in stores:
        copy.wait()


def early(sources, receivers):
    windows, parts, bins, width = sources[0].shape
    slot_rows = windows * parts
    met = len(receivers) * slot_rows
    rest = (len(sources) - len(receivers)) * slot_rows
    vmem = pl.BlockSpec(memory_space=pltpu.VMEM)
    lanes = width // LANES
    return pl.pallas_call(
        functools.partial(early_kernel, len(sources)),
        out_shape=(
            jax.ShapeDtypeStruct((bins, 2 * width, width), jnp.float32),
            jax.ShapeDtypeStruct((bins, 2 * width, rest), jnp.bfloat16),
        ),
        in_specs=[vmem] * (len(sources) + len(receivers)),
        out_specs=(vmem, vmem),
        scratch_shapes=[
            pltpu.VMEM((lanes, (met + rest) * bins, LANES), jnp.float32),
            pltpu.VMEM((lanes, (met + rest) * bins, LANES), jnp.float32),
            pltpu.VMEM((lanes, met * bins, LANES), jnp.float32),
        ],
        compiler_params=pltpu.CompilerParams(vmem_limit_bytes=40 * 2**20),
        cost_estimate=pl.CostEstimate(flops=1_000_000, bytes_accessed=1_000_000, transcendentals=0),
    )(*sources, *receivers)


def late(receivers, acc, left, scale):
    windows, parts, bins, width = receivers[0].shape[1:]
    vmem = pl.BlockSpec(memory_space=pltpu.VMEM)
    hbm = pl.BlockSpec(memory_space=pl.ANY)
    return pl.pallas_call(
        functools.partial(late_kernel, scale, len(receivers)),
        out_shape=jax.ShapeDtypeStruct((2, bins, width, width), jnp.bfloat16),
        in_specs=[vmem] * (len(receivers) + 2),
        out_specs=hbm,
        scratch_shapes=[
            pltpu.VMEM((width // LANES, left.shape[-1] * bins, LANES), jnp.float32),
            pltpu.VMEM((2, bins, width, width), jnp.bfloat16),
            pltpu.SemaphoreType.DMA((2, bins)),
        ],
        compiler_params=pltpu.CompilerParams(vmem_limit_bytes=40 * 2**20),
        cost_estimate=pl.CostEstimate(flops=200_000_000, bytes_accessed=9_000_000, transcendentals=200_000),
    )(*receivers, acc, left)


def pack_kernel(place_ref, source, z, p, y1, y2, y3, y4):
    place = place_ref[0, 0]
    pairs = (None, y1, y2, y3)
    for t in range(1, 8):
        out = y4 if t == 4 else pairs[t % 4].at[t // 4]

        def put(cond, ref, index, out=out):
            @pl.when(cond)
            def _():
                out[...] = ref[index]

        aside = {6: place == 0, 7: place == 2}.get(t, False)
        if t <= 3:
            put(place >= t, source, t)
        put((place < t) & (place >= t - 4), z, jnp.clip(t - 1 - place, 0, 3))
        if t in (6, 7):
            put(aside, source, t)
        if t in (5, 7):
            put(place == 0, p, t // 7)
        if t in (6, 7):
            put(place == 1, p, t - 6)


def pack(place, source, z, p):
    slot = jax.ShapeDtypeStruct(source.shape[1:], source.dtype)
    two = jax.ShapeDtypeStruct((2,) + source.shape[1:], source.dtype)
    vmem = pl.BlockSpec(memory_space=pltpu.VMEM)
    return pl.pallas_call(
        pack_kernel,
        out_shape=(two, two, two, slot),
        in_specs=[pl.BlockSpec(memory_space=pltpu.SMEM)] + [vmem] * 3,
        out_specs=(vmem,) * 4,
        compiler_params=pltpu.CompilerParams(vmem_limit_bytes=24 * 2**20),
        cost_estimate=pl.CostEstimate(flops=1_000, bytes_accessed=1_000, transcendentals=0),
    )(place.astype(jnp.int32).reshape(1, 1), source, z, p)


PLAN = (
    ("send", "W"),
    ("send", "Q"),
    ("send", "P"),
    ("send", "Z"),
    ("after", "Z"),
    ("after", "P"),
    ("after", "Q"),
    ("send", "F"),
)


def body(source_spectra, receiver_spectra):
    source, receiver = source_spectra[0], receiver_spectra[0]
    groups, windows = source.shape[:2]
    core = lax.axis_index("src") % 2
    place = lax.axis_index("rcv") % 4
    got = {}

    def of_core(zero, one):
        return jnp.where(core == 0, zero, one)

    def low(far):
        return of_core(receiver[1], receiver[3]) if far else of_core(receiver[3], receiver[1])

    def high(far):
        return of_core(receiver[5], receiver[7]) if far else of_core(receiver[7], receiver[5])

    def back(steps):
        return [(i, (i - steps(i)) % 16) for i in range(16)]

    def back_z(steps, places=range(4)):
        return [(i, (i - 4 * steps) % 32) for i in range(32) if i % 4 in places]

    def back_y(steps):
        return [(i, i // 4 * 4 + (i % 4 - steps) % 4) for i in range(32)]

    def nothing_like(*shapes):
        return lambda *_: tuple(jnp.zeros(s + receiver.shape[1:], receiver.dtype) for s in shapes)

    def one_x_step(receiver):
        x6 = lax.ppermute(receiver[6], "src", back(lambda i: 4))
        d = lax.ppermute(high(True), "src", [(i, (i - 4) % 16 ^ 1) for i in range(16)])
        first, x6 = lax.optimization_barrier((low(True), x6))
        cl = lax.ppermute(first, "src", [(i, i ^ 1) for i in range(16)])
        return x6, d, cl

    x6, d, cl = lax.cond(core < 2, one_x_step, nothing_like((), (), ()), receiver)
    across_y = [(i, i // 4 * 4 + {0: 2, 2: 3}[i % 4]) for i in range(32) if i % 2 == 0]

    moves = {
        "F": ("src", back(lambda i: 2), lambda: jnp.stack([receiver[2], x6, cl, d])),
        "Z": ("rcv", back_z(1), lambda: lax.dynamic_slice_in_dim(source, 1 + place, 4, 0)),
        "P": ("rcv", back_z(2, (0, 1)), lambda: jnp.stack([jnp.where(place == 0, source[5], source[6]), source[7]])),
        "W": ("rcv", across_y, lambda: jnp.where(place == 0, source[6], source[7])),
        "Q": ("rcv", back_z(2, (2, 3)), lambda: got["W"]),
    }
    tied = []
    for act, name in PLAN:
        if act == "after":
            tied.append(name)
            continue
        axis, route, make = moves[name]
        block = make()
        if tied:
            block, *arrived = lax.optimization_barrier((block, *[got[n] for n in tied]))
            got.update(zip(tied, arrived))
        got[name] = lax.ppermute(block, axis, route)

    def along_y(place, source, receiver, z, p):
        x2 = lax.ppermute(jnp.stack([receiver[4], high(False)]), "src", back(lambda i: 4))
        one, two, three, four = pack(place, source, z, p)
        pairs = [lax.ppermute(x, "rcv", back_y(b)) for b, x in ((1, one), (2, two), (3, three))]
        near = jnp.stack([low(False), x2[1]])
        near = lax.ppermute(near, "src", back(lambda i: 3 - 2 * (i % 2)))
        return (*pairs, four, x2[0], near)

    y1, y2, y3, four, x4, near = lax.cond(
        core < 2, along_y, nothing_like((2,), (2,), (2,), (), (), (2,)), place, source, receiver, got["Z"], got["P"]
    )
    two, three = jnp.where(place == 2, got["Q"], y2[1]), jnp.where(place == 3, got["Q"], y3[1])
    sources = [source[0], four, of_core(y1[0], y3[0]), of_core(y1[1], three)]
    sources += [y2[0], two, of_core(y3[0], y1[0]), of_core(three, y1[1])]
    acc, left = early(sources, [receiver[0], x4, near[0], near[1]])
    return late([got["F"]], acc, left, (groups * windows) ** (-0.5))


def solution(mesh):
    return jax.shard_map(
        body,
        mesh=mesh,
        in_specs=(P("rcv", None, None, None, None, "src"), P("src", None, None, None, None, "rcv")),
        out_specs=P(None, None, "src", "rcv"),
        check_vma=False,
    )
```

```python
import functools

import jax
import jax.numpy as jnp
from jax import lax
from jax.experimental import pallas as pl
from jax.experimental.pallas import tpu as pltpu
from jax.sharding import PartitionSpec as P


LANES = 128


def whiten_slot(slot_ref, first, out_ref, turned_ref=None):
    windows, parts, bins, width = slot_ref.shape

    def put(ref, row, values):
        for h in range(width // LANES):
            ref[h, pl.ds(row, bins), :] = values[:, h * LANES:(h + 1) * LANES]

    def one_window(w, carry):
        values = slot_ref[w].astype(jnp.float32)
        re, im = values[0], values[1]
        power = re * re + im * im
        level = jnp.mean(power, axis=0, keepdims=True)
        gain = lax.rsqrt(0.5 * power + 0.5 * level + 0.25)
        re, im = re * gain, im * gain
        row = pl.multiple_of(first + w * parts * bins, bins)
        put(out_ref, row, re)
        put(out_ref, row + bins, im)
        if turned_ref is not None:
            put(turned_ref, row, im)
            put(turned_ref, row + bins, -re)
        return carry

    lax.fori_loop(0, windows, one_window, 0, unroll=True)


def of_bin(ref, b, first, rows, bins):
    halves = [ref[h, pl.ds(first * bins + b, rows, stride=bins), :] for h in range(ref.shape[0])]
    return jnp.concatenate(halves, axis=-1)


def early_kernel(count, *refs):
    slots, (acc, left, u, t, v) = refs[:-5], refs[-5:]
    sources, receivers = slots[:count], slots[count:]
    windows, parts, bins, width = slots[0].shape
    slot_rows = windows * parts
    for k, ref in enumerate(sources):
        whiten_slot(ref, k * slot_rows * bins, u, t)
    for k, ref in enumerate(receivers):
        whiten_slot(ref, k * slot_rows * bins, v)
    met = len(receivers) * slot_rows
    rest = (len(sources) - len(receivers)) * slot_rows
    for b in range(bins):
        right = of_bin(v, b, 0, met, bins).astype(jnp.bfloat16)
        for part, ref in enumerate((u, t)):
            now = of_bin(ref, b, 0, met, bins).astype(jnp.bfloat16)
            acc[b, part * width:(part + 1) * width, :] = lax.dot_general(
                now, right, (((0,), (0,)), ((), ())), preferred_element_type=jnp.float32
            )
            later = of_bin(ref, b, met, rest, bins)
            left[b, part * width:(part + 1) * width, :] = later.T.astype(jnp.bfloat16)


def late_kernel(scale, count, *refs):
    slots = [ref.at[k] for ref in refs[:count] for k in range(ref.shape[0])]
    acc, left, out_hbm, v, block, out_sem = refs[count:]
    windows, parts, bins, width = slots[0].shape
    slot_rows = windows * parts
    for k, ref in enumerate(slots):
        whiten_slot(ref, k * slot_rows * bins, v)
    stores = []
    for b in range(bins):
        right = of_bin(v, b, 0, len(slots) * slot_rows, bins).astype(jnp.bfloat16)
        total = acc[b] + jnp.dot(left[b], right, preferred_element_type=jnp.float32)
        total = (total * scale).astype(jnp.bfloat16)
        block[0, b] = total[:width]
        block[1, b] = total[width:]
        for part in range(2):
            copy = pltpu.make_async_copy(block.at[part, b], out_hbm.at[part, b], out_sem.at[part, b])
            copy.start()
            stores.append(copy)
    for copy in stores:
        copy.wait()


def early(sources, receivers):
    windows, parts, bins, width = sources[0].shape
    slot_rows = windows * parts
    met = len(receivers) * slot_rows
    rest = (len(sources) - len(receivers)) * slot_rows
    vmem = pl.BlockSpec(memory_space=pltpu.VMEM)
    lanes = width // LANES
    return pl.pallas_call(
        functools.partial(early_kernel, len(sources)),
        out_shape=(
            jax.ShapeDtypeStruct((bins, 2 * width, width), jnp.float32),
            jax.ShapeDtypeStruct((bins, 2 * width, rest), jnp.bfloat16),
        ),
        in_specs=[vmem] * (len(sources) + len(receivers)),
        out_specs=(vmem, vmem),
        scratch_shapes=[
            pltpu.VMEM((lanes, (met + rest) * bins, LANES), jnp.float32),
            pltpu.VMEM((lanes, (met + rest) * bins, LANES), jnp.float32),
            pltpu.VMEM((lanes, met * bins, LANES), jnp.float32),
        ],
        compiler_params=pltpu.CompilerParams(vmem_limit_bytes=40 * 2**20),
        cost_estimate=pl.CostEstimate(flops=1_000_000, bytes_accessed=1_000_000, transcendentals=0),
    )(*sources, *receivers)


def late(receivers, acc, left, scale):
    windows, parts, bins, width = receivers[0].shape[1:]
    vmem = pl.BlockSpec(memory_space=pltpu.VMEM)
    hbm = pl.BlockSpec(memory_space=pl.ANY)
    return pl.pallas_call(
        functools.partial(late_kernel, scale, len(receivers)),
        out_shape=jax.ShapeDtypeStruct((2, bins, width, width), jnp.bfloat16),
        in_specs=[vmem] * (len(receivers) + 2),
        out_specs=hbm,
        scratch_shapes=[
            pltpu.VMEM((width // LANES, left.shape[-1] * bins, LANES), jnp.float32),
            pltpu.VMEM((2, bins, width, width), jnp.bfloat16),
            pltpu.SemaphoreType.DMA((2, bins)),
        ],
        compiler_params=pltpu.CompilerParams(vmem_limit_bytes=40 * 2**20),
        cost_estimate=pl.CostEstimate(flops=200_000_000, bytes_accessed=9_000_000, transcendentals=200_000),
    )(*receivers, acc, left)


def pack_kernel(place_ref, source, z, p, y1, y2, y3, y4):
    place = place_ref[0, 0]
    pairs = (None, y1, y2, y3)
    for t in range(1, 8):
        out = y4 if t == 4 else pairs[t % 4].at[t // 4]

        def put(cond, ref, index, out=out):
            @pl.when(cond)
            def _():
                out[...] = ref[index]

        aside = {6: place == 0, 7: place == 2}.get(t, False)
        if t <= 3:
            put(place >= t, source, t)
        put((place < t) & (place >= t - 4), z, jnp.clip(t - 1 - place, 0, 3))
        if t in (6, 7):
            put(aside, source, t)
        if t in (5, 7):
            put(place == 0, p, t // 7)
        if t in (6, 7):
            put(place == 1, p, t - 6)


def pack(place, source, z, p):
    slot = jax.ShapeDtypeStruct(source.shape[1:], source.dtype)
    two = jax.ShapeDtypeStruct((2,) + source.shape[1:], source.dtype)
    vmem = pl.BlockSpec(memory_space=pltpu.VMEM)
    return pl.pallas_call(
        pack_kernel,
        out_shape=(two, two, two, slot),
        in_specs=[pl.BlockSpec(memory_space=pltpu.SMEM)] + [vmem] * 3,
        out_specs=(vmem,) * 4,
        compiler_params=pltpu.CompilerParams(vmem_limit_bytes=24 * 2**20),
        cost_estimate=pl.CostEstimate(flops=1_000, bytes_accessed=1_000, transcendentals=0),
    )(place.astype(jnp.int32).reshape(1, 1), source, z, p)


def first_kernel(place_ref, source, z, p, w):
    place = place_ref[0, 0]
    for k in range(4):
        z[k] = source[1 + place + k]
    p[0] = source[jnp.minimum(5 + place, 6)]
    p[1] = source[7]
    w[...] = source[jnp.minimum(6 + place, 7)]


def first_blocks(place, source):
    shape = lambda *n: jax.ShapeDtypeStruct(n + source.shape[1:], source.dtype)
    vmem = pl.BlockSpec(memory_space=pltpu.VMEM)
    return pl.pallas_call(
        first_kernel,
        out_shape=(shape(4), shape(2), shape()),
        in_specs=[pl.BlockSpec(memory_space=pltpu.SMEM), vmem],
        out_specs=(vmem,) * 3,
        compiler_params=pltpu.CompilerParams(vmem_limit_bytes=24 * 2**20),
        cost_estimate=pl.CostEstimate(flops=0, bytes_accessed=3_000_000, transcendentals=0),
    )(place.astype(jnp.int32).reshape(1, 1), source)


PLAN = (
    ("send", "W"),
    ("send", "Q"),
    ("send", "P"),
    ("send", "Z"),
    ("after", "Z"),
    ("after", "P"),
    ("after", "Q"),
    ("send", "F"),
)


def body(source_spectra, receiver_spectra):
    source, receiver = source_spectra[0], receiver_spectra[0]
    groups, windows = source.shape[:2]
    core = lax.axis_index("src") % 2
    place = lax.axis_index("rcv") % 4
    got = {}

    def of_core(zero, one):
        return jnp.where(core == 0, zero, one)

    def low(far):
        return of_core(receiver[1], receiver[3]) if far else of_core(receiver[3], receiver[1])

    def high(far):
        return of_core(receiver[5], receiver[7]) if far else of_core(receiver[7], receiver[5])

    def back(steps):
        return [(i, (i - steps(i)) % 16) for i in range(16)]

    def back_z(steps, places=range(4)):
        return [(i, (i - 4 * steps) % 32) for i in range(32) if i % 4 in places]

    def back_y(steps):
        return [(i, i // 4 * 4 + (i % 4 - steps) % 4) for i in range(32)]

    def nothing_like(*shapes):
        return lambda *_: tuple(jnp.zeros(s + receiver.shape[1:], receiver.dtype) for s in shapes)

    def one_x_step(receiver):
        x6 = lax.ppermute(receiver[6], "src", back(lambda i: 4))
        d = lax.ppermute(high(True), "src", [(i, (i - 4) % 16 ^ 1) for i in range(16)])
        first, x6 = lax.optimization_barrier((low(True), x6))
        cl = lax.ppermute(first, "src", [(i, i ^ 1) for i in range(16)])
        return x6, d, cl

    x6, d, cl = lax.cond(core < 2, one_x_step, nothing_like((), (), ()), receiver)
    across_y = [(i, i // 4 * 4 + {0: 2, 2: 3}[i % 4]) for i in range(32) if i % 2 == 0]

    first_z, first_p, first_w = first_blocks(place, source)
    moves = {
        "F": ("src", back(lambda i: 2), lambda: jnp.stack([receiver[2], x6, cl, d])),
        "Z": ("rcv", back_z(1), lambda: first_z),
        "P": ("rcv", back_z(2, (0, 1)), lambda: first_p),
        "W": ("rcv", across_y, lambda: first_w),
        "Q": ("rcv", back_z(2, (2, 3)), lambda: got["W"]),
    }
    tied = []
    for act, name in PLAN:
        if act == "after":
            tied.append(name)
            continue
        axis, route, make = moves[name]
        block = make()
        if tied:
            block, *arrived = lax.optimization_barrier((block, *[got[n] for n in tied]))
            got.update(zip(tied, arrived))
        got[name] = lax.ppermute(block, axis, route)

    def along_y(place, source, receiver, z, p):
        x2 = lax.ppermute(jnp.stack([receiver[4], high(False)]), "src", back(lambda i: 4))
        one, two, three, four = pack(place, source, z, p)
        pairs = [lax.ppermute(x, "rcv", back_y(b)) for b, x in ((1, one), (2, two), (3, three))]
        near = jnp.stack([low(False), x2[1]])
        near = lax.ppermute(near, "src", back(lambda i: 3 - 2 * (i % 2)))
        return (*pairs, four, x2[0], near)

    y1, y2, y3, four, x4, near = lax.cond(
        core < 2, along_y, nothing_like((2,), (2,), (2,), (), (), (2,)), place, source, receiver, got["Z"], got["P"]
    )
    two, three = jnp.where(place == 2, got["Q"], y2[1]), jnp.where(place == 3, got["Q"], y3[1])
    sources = [source[0], four, of_core(y1[0], y3[0]), of_core(y1[1], three)]
    sources += [y2[0], two, of_core(y3[0], y1[0]), of_core(three, y1[1])]
    acc, left = early(sources, [receiver[0], x4, near[0], near[1]])
    return late([got["F"]], acc, left, (groups * windows) ** (-0.5))


def solution(mesh):
    return jax.shard_map(
        body,
        mesh=mesh,
        in_specs=(P("rcv", None, None, None, None, "src"), P("src", None, None, None, None, "rcv")),
        out_specs=P(None, None, "src", "rcv"),
        check_vma=False,
    )
```
